1024 devices in a mesh: dp: 16 (over z), expert: 64 (over x, y, core).
Axes of the slice: x: 4, y: 8, z: 16, core: 2. Of those that a mesh axis runs over, the one named last changes fastest.
Arguments:
- tokens: bfloat16 [2048, 4096], P('expert', 'dp'), may hold values from -6 to 6
- routes: int32 [2048, 8], P('expert'), may hold values from 0 to 63, all different within a row; in each aligned block of 32 rows (0 to 31, 32 to 63, ...) at most 8 rows name the same one
- gates: float32 [2048, 8], P('expert'), may hold values from 0.1 to 1
- counts: int32 [64], replicated, may hold values from 1 to 8
- w_gate_up: bfloat16 [64, 4096, 2, 1024], P('expert', 'dp'), may hold values from -0.09375 to 0.09375
- w_down: bfloat16 [64, 4096, 1024], P('expert', 'dp'), may hold values from -0.1875 to 0.1875
- cotangent: bfloat16 [2048, 4096], P('expert', 'dp'), may hold values from -6 to 6
Outputs:
- mixed: bfloat16 [2048, 4096], P('expert', 'dp')
- gate_grad: float32 [2048, 8], P('expert')
- token_grad: bfloat16 [2048, 4096], P('expert', 'dp')
- weight_grads: bfloat16 [64, 4096, 3, 1024], P('expert', 'dp')
The draws below stay inside these ranges and needn't reach their ends.
Inputs may be any that keep to these rules, and one draw needn't show every extreme that they name: `routes`: each token names 8 different experts; within the tokens of one group (32 tokens in a row from the start) no expert is named more than 8 times, a bound that some block reaches.
All inputs are finite; a program needn't handle non-finite values.
Results may differ from the reference program's by a relative error of at most 0.0064.
Values may be sent and summed in bfloat16 or wider, within the bound.
No kernel may reach another device: no remote copies, remote signals or barrier semaphores. Data moves between devices by JAX's collectives and lax.ppermute only.
A program may use at most 32 MiB of HBM per device.

```python
import math
import jax
import jax.numpy as jnp
import numpy as np
from jax import lax

D = 4096
FF = 1024
TOP = 8
TOK_DEV = 32
EXPERTS = 64
CAP = 8
TOKENS = 2048
N_EXPERT = 64


def set_ends(values, own_key, smallest, top_value):
    index_at = [jax.random.randint(jax.random.fold_in(own_key, axis), (), 0, length) for axis, length in enumerate(values.shape)]
    longest = values.shape.index(max(values.shape))
    next_to = index_at[:longest] + [(index_at[longest] + 1) % values.shape[longest]] + index_at[longest + 1:]
    return values.at[tuple(index_at)].set(smallest).at[tuple(next_to)].set(top_value)


def block_levels(own_key, dims, cuts, least, largest):
    gain = 1.0
    for position, shards_of in cuts:
        heights = jax.random.uniform(jax.random.fold_in(jax.random.fold_in(own_key, 6), position), (shards_of,), jnp.float32, least / len(cuts), largest / len(cuts))
        gain = gain * jnp.repeat(jnp.exp(heights), dims[position] // shards_of).reshape((-1,) + (1,) * (len(dims) - 1 - position))
    return gain


def routed_block(rng, own, number, rows, amount, top, bound, skew):
    sequence = jax.random.permutation(rng, amount)
    heavy_load, common = load_shares(amount, rows * top, bound, skew, True), load_shares(amount, rows * top, bound, skew, False)
    places = jnp.arange(amount)

    def named(sizes, offset_by):
        used = int((sizes > 0).sum())
        fixed = max(1, used // 4)
        shifted = fixed + (places - fixed + offset_by * (used - fixed)) % max(1, amount - fixed)
        return jnp.zeros((amount,), jnp.int32).at[sequence[jnp.where(places < fixed, places, shifted)]].set(jnp.asarray(sizes, jnp.int32))

    sizes = jnp.where(number % 4 == 0, named(heavy_load, number // 4), named(common, number - number // 4 - 1))
    mixed = jax.random.permutation(jax.random.fold_in(own, 3), amount)
    source_of, sink = mixed[0:amount // 2 * 2:2], mixed[1:amount // 2 * 2:2]
    slack = jnp.minimum(sizes[source_of] - 1, bound - sizes[sink]) // 2
    slack = jnp.where((source_of == sequence[0]) | (sink == sequence[0]) | (sizes[sink] == 0), 0, jnp.maximum(slack, 0))
    shifted = jax.random.randint(jax.random.fold_in(own, 4), (amount // 2,), 0, 1 << 20) % (slack + 1)
    sizes = sizes.at[source_of].add(-shifted).at[sink].add(shifted)
    items = jnp.searchsorted(jnp.cumsum(sizes), jnp.arange(rows * top), side="right").astype(jnp.int32)
    listing = items.reshape(top, rows).T
    listing = listing[jax.random.permutation(jax.random.fold_in(own, 1), rows)]
    offset_by = jax.random.randint(jax.random.fold_in(own, 2), (rows, 1), 0, top)
    return jnp.take_along_axis(listing, (jnp.arange(top)[None, :] + offset_by) % top, axis=1)


def load_shares(number_of, total, most, slope, full):
    loads = [(1 << 20) // math.isqrt(grade ** slope) + 1 for grade in range(1, number_of + 1)]
    largest = most if full else min(most, max(-(-total // number_of), total * loads[0] // sum(loads)))
    least = 1 if total - largest >= number_of - 1 else 0
    holding, rest = [largest] + [least] * (number_of - 1), total - largest - least * (number_of - 1)
    while rest > 0:
        movable = [i for i in range(1, number_of) if holding[i] < largest] or [i for i in range(1, number_of) if holding[i] < most]
        mass, remaining = sum([loads[i] for i in movable]), rest
        for i in movable:
            extra = min(most - holding[i], max(1, remaining * loads[i] // mass), rest)
            holding[i] = holding[i] + extra
            rest = rest - extra
    return np.array(holding)


def centred(rng, shape, scale, bound, shards=(), kind=jnp.bfloat16):
    array = scale * jax.random.normal(rng, shape, jnp.float32)
    if shards:
        array = array * block_levels(rng, shape, shards, -0.22, 0.18)
    return jnp.clip(array, -bound, bound).astype(kind)


def setup_inputs(seed: int = 0) -> dict:
    seeds = jax.random.split(jax.random.key(seed), 8)
    tokens = centred(seeds[0], (TOKENS, D), 1.0, 6.0, ((0, 64), (1, 16)))
    routes_keys = jax.random.split(jax.random.fold_in(seeds[1], 1), TOKENS // TOK_DEV)
    routes_turns = jax.random.permutation(jax.random.fold_in(seeds[1], 3), TOKENS // TOK_DEV)
    routes = jax.vmap(lambda own, number: routed_block(jax.random.fold_in(seeds[1], 2), own, number, TOK_DEV, EXPERTS, TOP, CAP, 1))(routes_keys, routes_turns).reshape((TOKENS, TOP))
    gates = jnp.clip(0.1 + 0.9 * jax.random.uniform(seeds[2], (TOKENS, TOP), jnp.float32) ** block_levels(seeds[2], (TOKENS, TOP), ((0, 64),), -0.2, 0.2), 0.1, 1.0)
    counts = set_ends(jax.random.randint(seeds[3], (N_EXPERT,), 1, 9), jax.random.fold_in(seeds[3], 1), 1, 8).astype(jnp.int32)
    w_gate_up = centred(seeds[4], (EXPERTS, D, 2, FF), D ** -0.5, 0.09375, ((0, 64), (1, 16)))
    w_down = centred(seeds[5], (EXPERTS, D, FF), FF ** -0.5, 0.1875, ((0, 64), (1, 16)))
    cotangent = centred(seeds[6], (TOKENS, D), 1.0, 6.0, ((0, 64), (1, 16)))
    return {"tokens": tokens, "routes": routes, "gates": gates, "counts": counts, "w_gate_up": w_gate_up, "w_down": w_down, "cotangent": cotangent}


def reference(tokens, routes, gates, counts, w_gate_up, w_down, cotangent):
    per_group = routes.reshape(N_EXPERT, TOK_DEV * TOP)
    member = (per_group[:, :, None] == jnp.arange(EXPERTS, dtype=jnp.int32)[None, None, :]).astype(jnp.int32)
    before = jnp.sum((jnp.cumsum(member, axis=1) - 1) * member, axis=2).astype(jnp.int32)
    flat_index = jnp.arange(N_EXPERT * TOK_DEV * TOP, dtype=jnp.int32).reshape(N_EXPERT, TOK_DEV * TOP)
    source = jnp.broadcast_to(jnp.arange(N_EXPERT, dtype=jnp.int32)[:, None], per_group.shape)
    table = jnp.full((EXPERTS, N_EXPERT, CAP), -1, jnp.int32).at[per_group, source, before].set(flat_index)
    shares = counts.astype(jnp.float32) / jnp.sum(counts.astype(jnp.float32))
    slot_share = jnp.repeat(shares, CAP)
    gate_flat = gates.reshape(-1)

    def expert_pass(carry, inputs):
        mixed_acc, gate_acc, grad_acc = carry
        index_rows, pair_full, down_weight = inputs
        pair_weight = pair_full.reshape(D, 2 * FF)
        row_index = index_rows.reshape(-1)
        is_live = row_index >= 0
        safe_index = jnp.where(is_live, row_index, 0).astype(jnp.int32)
        token_index = (safe_index // TOP).astype(jnp.int32)
        rows_in = jnp.where(is_live[:, None], tokens[token_index], jnp.zeros((), jnp.bfloat16))
        gate_up = jnp.dot(rows_in, pair_weight, preferred_element_type=jnp.float32).reshape(-1, 2, FF)
        gate_part = gate_up[:, 0, :]
        up_part = gate_up[:, 1, :]
        sig_gate = jax.nn.sigmoid(gate_part)
        silu_gate = gate_part * sig_gate
        hidden = (silu_gate * up_part).astype(jnp.bfloat16)
        expert_out = jnp.dot(hidden, down_weight.T, preferred_element_type=jnp.float32).astype(jnp.bfloat16)
        out_value = expert_out.astype(jnp.float32)
        gate_value = gate_flat[safe_index]
        incoming = cotangent[token_index].astype(jnp.float32)
        mixed_acc = mixed_acc.at[token_index].add(jnp.where(is_live[:, None], gate_value[:, None] * out_value, 0.0))
        gate_acc = gate_acc.at[safe_index].add(jnp.where(is_live, jnp.sum(incoming * out_value, axis=1), 0.0))
        out_grad = jnp.where(is_live[:, None], gate_value[:, None] * incoming, 0.0).astype(jnp.bfloat16)
        hidden_grad = jnp.dot(out_grad, down_weight, preferred_element_type=jnp.float32)
        slope_term = sig_gate * (1.0 + gate_part * (1.0 - sig_gate))
        pair_grad = jnp.stack([hidden_grad * up_part * slope_term, hidden_grad * silu_gate], axis=1).astype(jnp.bfloat16)
        pair_flat = pair_grad.reshape(-1, 2 * FF)
        row_grad = jnp.dot(pair_flat, pair_weight.T, preferred_element_type=jnp.float32).astype(jnp.bfloat16)
        grad_acc = grad_acc.at[token_index].add(jnp.where(is_live[:, None], row_grad.astype(jnp.float32), 0.0))
        weighted_pair = (slot_share[:, None] * pair_flat.astype(jnp.float32)).astype(jnp.bfloat16)
        weighted_hidden = (slot_share[:, None] * hidden.astype(jnp.float32)).astype(jnp.bfloat16)
        pair_update = jnp.dot(rows_in.T, weighted_pair, preferred_element_type=jnp.float32).reshape(D, 2, FF)
        down_update = jnp.dot(out_grad.T, weighted_hidden, preferred_element_type=jnp.float32)
        grads = jnp.concatenate([pair_update, down_update[:, None, :]], axis=1).astype(jnp.bfloat16)
        return (mixed_acc, gate_acc, grad_acc), grads

    start = (jnp.zeros((TOKENS, D), jnp.float32), jnp.zeros((TOKENS * TOP,), jnp.float32), jnp.zeros((TOKENS, D), jnp.float32))
    final, weight_grads = lax.scan(expert_pass, start, (table, w_gate_up, w_down))
    mixed_acc, gate_acc, grad_acc = final
    return mixed_acc.astype(jnp.bfloat16), gate_acc.reshape(TOKENS, TOP), grad_acc.astype(jnp.bfloat16), weight_grads
```

```python
import jax
import jax.numpy as jnp
from jax import lax
from jax.sharding import PartitionSpec as P

F32 = jnp.float32
BF16 = jnp.bfloat16


def shards(tokens, routes, gates, counts, w_gate_up, w_down, cotangent):
    experts = lax.axis_size("expert")
    rows, width = tokens.shape
    top = routes.shape[1]
    cap = min(rows, 2 * rows * top // experts)
    slots = experts * cap
    ff = w_down.shape[2]
    pair_weight = w_gate_up[0]
    down_weight = w_down[0]

    slot_id = jnp.arange(slots, dtype=jnp.int32)
    slot_expert = slot_id // cap
    slot_pos = slot_id % cap
    named = routes[:, :, None] == slot_expert[None, None, :]
    member = jnp.any(named, axis=1).astype(BF16)
    earlier = jnp.tril(jnp.ones((rows, rows), BF16), -1)
    before = jnp.dot(earlier, member, preferred_element_type=F32)
    place = jnp.where(before == slot_pos[None, :].astype(F32), member, jnp.zeros((), BF16))
    gate_of = jnp.sum(jnp.where(named, gates[:, :, None], 0.0), axis=1) * place.astype(F32)
    gate_slot = jnp.sum(gate_of, axis=0)

    both = jnp.concatenate([tokens, cotangent], axis=1)
    picked = lax.dot_general(place, both, (((0,), (0,)), ((), ())), preferred_element_type=F32)
    scale = jnp.where(jnp.arange(2 * width)[None, :] < width, 1.0, gate_slot[:, None])
    outgoing = (picked * scale).astype(BF16).reshape(experts, cap, 2 * width)
    arrived = lax.all_to_all(outgoing, "expert", split_axis=0, concat_axis=0, tiled=True)
    arrived = arrived.reshape(slots, 2 * width)
    rows_in = arrived[:, :width]
    grad_rows = arrived[:, width:]

    pair_part = lax.dot_general(
        pair_weight, rows_in, (((0,), (1,)), ((), ())), preferred_element_type=F32
    )
    hidden_grad_part = lax.dot_general(
        down_weight, grad_rows, (((0,), (1,)), ((), ())), preferred_element_type=F32
    )
    ranks = lax.axis_size("dp")
    part_ff = ff // ranks
    part = jnp.concatenate([pair_part, hidden_grad_part[None]], axis=0)
    part = part.reshape(3, ranks, part_ff, slots).transpose(1, 0, 2, 3)
    part = part.reshape(3 * ff, slots)
    sums = lax.psum_scatter(part, "dp", scatter_dimension=0, tiled=True)
    gate_part = sums[:part_ff]
    up_part = sums[part_ff : 2 * part_ff]
    hidden_grad = sums[2 * part_ff :]
    sig_gate = jax.nn.sigmoid(gate_part)
    silu_gate = gate_part * sig_gate
    hidden_value = silu_gate * up_part
    slope_term = sig_gate * (1.0 + gate_part * (1.0 - sig_gate))
    gate_dot = jnp.sum(hidden_value * hidden_grad, axis=0)
    dot_hi = gate_dot.astype(BF16)
    dot_lo = (gate_dot - dot_hi.astype(F32)).astype(BF16)
    extra = jnp.concatenate(
        [dot_hi[None], dot_lo[None], jnp.zeros((14, slots), BF16)], axis=0
    )
    payload = jnp.concatenate(
        [
            hidden_value.astype(BF16),
            (hidden_grad * up_part * slope_term).astype(BF16),
            (hidden_grad * silu_gate).astype(BF16),
            extra,
        ],
        axis=0,
    )
    full = lax.all_gather(payload, "dp", axis=0, tiled=False)
    hidden_full = full[:, :part_ff].reshape(ff, slots)
    gate_grad_full = full[:, part_ff : 2 * part_ff].reshape(ff, slots)
    up_grad_full = full[:, 2 * part_ff : 3 * part_ff].reshape(ff, slots)
    pair_full = jnp.stack([gate_grad_full, up_grad_full], axis=0)
    dots = full[:, 3 * part_ff : 3 * part_ff + 2]
    dot_slot = jnp.sum(dots.astype(F32), axis=(0, 1))

    expert_out = lax.dot_general(
        hidden_full, down_weight, (((0,), (1,)), ((), ())), preferred_element_type=F32
    ).astype(BF16)
    row_grad = lax.dot_general(
        pair_full, pair_weight, (((0, 1), (1, 2)), ((), ())), preferred_element_type=F32
    ).astype(BF16)
    slot_hi = dot_slot.astype(BF16)
    slot_lo = (dot_slot - slot_hi.astype(F32)).astype(BF16)
    tail = jnp.concatenate(
        [slot_hi[:, None], slot_lo[:, None], jnp.zeros((slots, 126), BF16)], axis=1
    )
    back = jnp.concatenate([expert_out, row_grad, tail], axis=1)
    returned = lax.all_to_all(
        back.reshape(experts, cap, 2 * width + 128),
        "expert",
        split_axis=0,
        concat_axis=0,
        tiled=True,
    ).reshape(slots, 2 * width + 128)

    shares = counts.astype(F32) / jnp.sum(counts.astype(F32))
    slot_share = jnp.repeat(shares, cap)
    weighted_pair = (slot_share[None, None, :] * pair_full.astype(F32)).astype(BF16)
    weighted_hidden = (slot_share[None, :] * hidden_full.astype(F32)).astype(BF16)
    pair_update = lax.dot_general(
        rows_in, weighted_pair, (((0,), (2,)), ((), ())), preferred_element_type=F32
    ).astype(BF16)
    down_update = lax.dot_general(
        grad_rows, weighted_hidden, (((0,), (1,)), ((), ())), preferred_element_type=F32
    ).astype(BF16)
    weight_grads = jnp.concatenate([pair_update, down_update[:, None, :]], axis=1)

    gate_hi = gate_of.astype(BF16)
    gate_lo = (gate_of - gate_hi.astype(F32)).astype(BF16)
    combine = jnp.concatenate([gate_hi, gate_lo], axis=0)
    mixed_parts = jnp.dot(combine, returned[:, :width], preferred_element_type=F32)
    mixed = (mixed_parts[:rows] + mixed_parts[rows:]).astype(BF16)
    token_grad = jnp.dot(
        place, returned[:, width : 2 * width], preferred_element_type=F32
    ).astype(BF16)
    dot_back = jnp.sum(returned[:, 2 * width : 2 * width + 2].astype(F32), axis=1)
    at_slot = place.astype(F32) * dot_back[None, :]
    gate_grad = jnp.sum(jnp.where(named, at_slot[:, None, :], 0.0), axis=2) / gates
    return (mixed, gate_grad, token_grad, weight_grads[None])


def solution(mesh):
    return jax.shard_map(
        shards,
        mesh=mesh,
        in_specs=(
            P("expert", "dp"),
            P("expert", None),
            P("expert", None),
            P(),
            P("expert", "dp", None, None),
            P("expert", "dp", None),
            P("expert", "dp"),
        ),
        out_specs=(
            P("expert", "dp"),
            P("expert", None),
            P("expert", "dp"),
            P("expert", "dp", None, None),
        ),
        check_vma=False,
    )
```

```python
import jax
import jax.numpy as jnp
from jax import lax
from jax.sharding import PartitionSpec as P

F32 = jnp.float32
BF16 = jnp.bfloat16


def shards(tokens, routes, gates, counts, w_gate_up, w_down, cotangent):
    experts = lax.axis_size("expert")
    rows, width = tokens.shape
    top = routes.shape[1]
    cap = min(rows, 2 * rows * top // experts)
    slots = experts * cap
    ff = w_down.shape[2]
    pair_weight = w_gate_up[0]
    down_weight = w_down[0]

    slot_id = jnp.arange(slots, dtype=jnp.int32)
    slot_expert = slot_id // cap
    slot_pos = slot_id % cap
    named = routes[:, :, None] == slot_expert[None, None, :]
    member = jnp.any(named, axis=1).astype(BF16)
    earlier = jnp.tril(jnp.ones((rows, rows), BF16), -1)
    before = jnp.dot(earlier, member, preferred_element_type=F32)
    place = jnp.where(before == slot_pos[None, :].astype(F32), member, jnp.zeros((), BF16))
    gate_of = jnp.sum(jnp.where(named, gates[:, :, None], 0.0), axis=1) * place.astype(F32)
    gate_slot = jnp.sum(gate_of, axis=0)

    both = jnp.concatenate([tokens, cotangent], axis=1)
    picked = lax.dot_general(place, both, (((0,), (0,)), ((), ())), preferred_element_type=F32)
    scale = jnp.where(jnp.arange(2 * width)[None, :] < width, 1.0, gate_slot[:, None])
    outgoing = (picked * scale).astype(BF16).reshape(experts, cap, 2 * width)
    arrived = lax.all_to_all(outgoing, "expert", split_axis=0, concat_axis=0, tiled=True)
    arrived = arrived.reshape(slots, 2 * width)
    rows_in = arrived[:, :width]
    grad_rows = arrived[:, width:]

    pair_part = lax.dot_general(
        rows_in, pair_weight, (((1,), (0,)), ((), ())), preferred_element_type=F32
    )
    hidden_grad_part = jnp.dot(grad_rows, down_weight, preferred_element_type=F32)
    part = jnp.concatenate([pair_part, hidden_grad_part[:, None, :]], axis=1)
    sums = lax.psum_scatter(part, "dp", scatter_dimension=0, tiled=True)
    gate_part, up_part, hidden_grad = sums[:, 0], sums[:, 1], sums[:, 2]
    sig_gate = jax.nn.sigmoid(gate_part)
    silu_gate = gate_part * sig_gate
    hidden_value = silu_gate * up_part
    slope_term = sig_gate * (1.0 + gate_part * (1.0 - sig_gate))
    gate_dot = jnp.sum(hidden_value * hidden_grad, axis=1)
    hidden = hidden_value.astype(BF16)
    gate_grad_part = (hidden_grad * up_part * slope_term).astype(BF16)
    up_grad_part = (hidden_grad * silu_gate).astype(BF16)
    later_weight, _ = lax.optimization_barrier((pair_weight, part))
    flat_weight = later_weight.reshape(width, 2 * ff)

    ranks = lax.axis_size("dp")
    half = ranks // 2
    same_parity = [[2 * i + q for i in range(half)] for q in range(2)]
    to_right = [(i, (i + 1) % ranks) for i in range(ranks)]
    to_left = [(i, (i - 1) % ranks) for i in range(ranks)]
    is_even = lax.axis_index("dp") % 2 == 0

    def gather(value):
        own = lax.all_gather(value, "dp", axis=0, tiled=False, axis_index_groups=same_parity)
        first = lax.ppermute(own[: half // 2], "dp", to_right)
        second = lax.ppermute(own[half // 2 :], "dp", to_left)
        other = jnp.concatenate([first, second], axis=0)
        even = jnp.where(is_even, own, other)
        odd = jnp.where(is_even, other, own)
        return jnp.stack([even, odd], axis=1).reshape(slots, value.shape[1])

    dot_hi = gate_dot.astype(BF16)
    dot_lo = (gate_dot - dot_hi.astype(F32)).astype(BF16)
    lane = jnp.arange(128)[None, :]
    dots = jnp.where(lane == 0, dot_hi[:, None], jnp.where(lane == 1, dot_lo[:, None], jnp.zeros((), BF16)))
    gathered = gather(jnp.concatenate([hidden, dots], axis=1))
    hidden_full = gathered[:, :ff]
    gate_grad_full = gather(gate_grad_part)
    up_grad_full = gather(up_grad_part)

    expert_out = lax.dot_general(
        hidden_full, down_weight, (((1,), (1,)), ((), ())), preferred_element_type=F32
    ).astype(BF16)
    row_grad = (
        lax.dot_general(
            gate_grad_full, flat_weight[:, :ff], (((1,), (1,)), ((), ())), preferred_element_type=F32
        )
        + lax.dot_general(
            up_grad_full, flat_weight[:, ff:], (((1,), (1,)), ((), ())), preferred_element_type=F32
        )
    ).astype(BF16)

    def send_back(value):
        sent = value.reshape(experts, cap, value.shape[1])
        came = lax.all_to_all(sent, "expert", split_axis=0, concat_axis=0, tiled=True)
        return came.reshape(slots, value.shape[1])

    first_back = send_back(jnp.concatenate([expert_out, gathered[:, ff:]], axis=1))
    grad_back = send_back(row_grad)
    out_back = first_back[:, :width]
    dot_back = jnp.sum(first_back[:, width:].astype(F32), axis=1)
    at_slot = place.astype(F32) * dot_back[None, :]
    gate_grad = jnp.sum(jnp.where(named, at_slot[:, None, :], 0.0), axis=2) / gates

    shares = counts.astype(F32) / jnp.sum(counts.astype(F32))
    slot_share = jnp.repeat(shares, cap)[:, None]
    weighted_gate = (slot_share * gate_grad_full.astype(F32)).astype(BF16)
    weighted_up = (slot_share * up_grad_full.astype(F32)).astype(BF16)
    weighted_hidden = (slot_share * hidden_full.astype(F32)).astype(BF16)
    gate_update = lax.dot_general(
        rows_in, weighted_gate, (((0,), (0,)), ((), ())), preferred_element_type=F32
    ).astype(BF16)
    up_update = lax.dot_general(
        rows_in, weighted_up, (((0,), (0,)), ((), ())), preferred_element_type=F32
    ).astype(BF16)
    down_update = lax.dot_general(
        grad_rows, weighted_hidden, (((0,), (0,)), ((), ())), preferred_element_type=F32
    ).astype(BF16)
    weight_grads = jnp.stack([gate_update, up_update, down_update], axis=1)

    gate_hi = gate_of.astype(BF16)
    gate_lo = (gate_of - gate_hi.astype(F32)).astype(BF16)
    combine = jnp.concatenate([gate_hi, gate_lo], axis=0)
    mixed_parts = jnp.dot(combine, out_back, preferred_element_type=F32)
    mixed = (mixed_parts[:rows] + mixed_parts[rows:]).astype(BF16)
    token_grad = jnp.dot(place, grad_back, preferred_element_type=F32).astype(BF16)
    return (mixed, gate_grad, token_grad, weight_grads[None])


def solution(mesh):
    return jax.shard_map(
        shards,
        mesh=mesh,
        in_specs=(
            P("expert", "dp"),
            P("expert", None),
            P("expert", None),
            P(),
            P("expert", "dp", None, None),
            P("expert", "dp", None),
            P("expert", "dp"),
        ),
        out_specs=(
            P("expert", "dp"),
            P("expert", None),
            P("expert", "dp"),
            P("expert", "dp", None, None),
        ),
        check_vma=False,
    )
```

```python
import jax
import jax.numpy as jnp
from jax import lax
from jax.sharding import PartitionSpec as P

F32 = jnp.float32
BF16 = jnp.bfloat16


def shards(tokens, routes, gates, counts, w_gate_up, w_down, cotangent):
    experts = lax.axis_size("expert")
    rows, width = tokens.shape
    top = routes.shape[1]
    cap = min(rows, 2 * rows * top // experts)
    slots = experts * cap
    ff = w_down.shape[2]
    pair_weight = w_gate_up[0]
    down_weight = w_down[0]

    slot_id = jnp.arange(slots, dtype=jnp.int32)
    slot_expert = slot_id // cap
    slot_pos = slot_id % cap
    named = routes[:, :, None] == slot_expert[None, None, :]
    member = jnp.any(named, axis=1).astype(BF16)
    earlier = jnp.tril(jnp.ones((rows, rows), BF16), -1)
    before = jnp.dot(earlier, member, preferred_element_type=F32)
    place = jnp.where(before == slot_pos[None, :].astype(F32), member, jnp.zeros((), BF16))
    gate_of = jnp.sum(jnp.where(named, gates[:, :, None], 0.0), axis=1) * place.astype(F32)
    gate_slot = jnp.sum(gate_of, axis=0)

    both = jnp.concatenate([tokens, cotangent], axis=1)
    picked = lax.dot_general(place, both, (((0,), (0,)), ((), ())), preferred_element_type=F32)
    scale = jnp.where(jnp.arange(2 * width)[None, :] < width, 1.0, gate_slot[:, None])
    outgoing = (picked * scale).astype(BF16).reshape(experts, cap, 2 * width)
    arrived = lax.all_to_all(outgoing, "expert", split_axis=0, concat_axis=0, tiled=True)
    arrived = arrived.reshape(slots, 2 * width)
    rows_in = arrived[:, :width]
    grad_rows = arrived[:, width:]

    pair_part = lax.dot_general(
        rows_in, pair_weight, (((1,), (0,)), ((), ())), preferred_element_type=F32
    )
    hidden_grad_part = jnp.dot(grad_rows, down_weight, preferred_element_type=F32)
    part = jnp.concatenate([pair_part, hidden_grad_part[:, None, :]], axis=1)
    sums = lax.psum_scatter(part, "dp", scatter_dimension=0, tiled=True)
    gate_part, up_part, hidden_grad = sums[:, 0], sums[:, 1], sums[:, 2]
    sig_gate = jax.nn.sigmoid(gate_part)
    silu_gate = gate_part * sig_gate
    hidden_value = silu_gate * up_part
    slope_term = sig_gate * (1.0 + gate_part * (1.0 - sig_gate))
    gate_dot = jnp.sum(hidden_value * hidden_grad, axis=1)
    hidden = hidden_value.astype(BF16)
    gate_grad_part = (hidden_grad * up_part * slope_term).astype(BF16)
    up_grad_part = (hidden_grad * silu_gate).astype(BF16)
    later_weight, _ = lax.optimization_barrier((pair_weight, part))
    flat_weight = later_weight.reshape(width, 2 * ff)
    full = lax.all_gather(
        jnp.concatenate([hidden, gate_grad_part, up_grad_part], axis=1), "dp", axis=0, tiled=True
    )
    hidden_full = full[:, :ff]
    pair_full = full[:, ff:]
    dots = lax.all_gather(gate_dot, "dp", axis=0, tiled=True)
    dot_back = lax.all_to_all(
        dots.reshape(experts, cap), "expert", split_axis=0, concat_axis=0, tiled=True
    ).reshape(slots)
    at_slot = place.astype(F32) * dot_back[None, :]
    gate_grad = jnp.sum(jnp.where(named, at_slot[:, None, :], 0.0), axis=2) / gates

    expert_out = lax.dot_general(
        hidden_full, down_weight, (((1,), (1,)), ((), ())), preferred_element_type=F32
    ).astype(BF16)
    row_grad = lax.dot_general(
        pair_full, flat_weight, (((1,), (1,)), ((), ())), preferred_element_type=F32
    ).astype(BF16)
    back = jnp.concatenate([expert_out, row_grad], axis=1)
    returned = lax.all_to_all(
        back.reshape(experts, cap, 2 * width), "expert", split_axis=0, concat_axis=0, tiled=True
    ).reshape(slots, 2 * width)
    out_back = returned[:, :width]
    grad_back = returned[:, width:]

    shares = counts.astype(F32) / jnp.sum(counts.astype(F32))
    slot_share = jnp.repeat(shares, cap)[:, None]
    weighted_pair = (slot_share * pair_full.astype(F32)).astype(BF16)
    weighted_hidden = (slot_share * hidden_full.astype(F32)).astype(BF16)
    gate_update = lax.dot_general(
        rows_in, weighted_pair[:, :ff], (((0,), (0,)), ((), ())), preferred_element_type=F32
    ).astype(BF16)
    up_update = lax.dot_general(
        rows_in, weighted_pair[:, ff:], (((0,), (0,)), ((), ())), preferred_element_type=F32
    ).astype(BF16)
    down_update = lax.dot_general(
        grad_rows, weighted_hidden, (((0,), (0,)), ((), ())), preferred_element_type=F32
    ).astype(BF16)
    weight_grads = jnp.stack([gate_update, up_update, down_update], axis=1)

    gate_hi = gate_of.astype(BF16)
    gate_lo = (gate_of - gate_hi.astype(F32)).astype(BF16)
    combine = jnp.concatenate([gate_hi, gate_lo], axis=0)
    mixed_parts = jnp.dot(combine, out_back, preferred_element_type=F32)
    mixed = (mixed_parts[:rows] + mixed_parts[rows:]).astype(BF16)
    token_grad = jnp.dot(place, grad_back, preferred_element_type=F32).astype(BF16)
    return (mixed, gate_grad, token_grad, weight_grads[None])


def solution(mesh):
    return jax.shard_map(
        shards,
        mesh=mesh,
        in_specs=(
            P("expert", "dp"),
            P("expert", None),
            P("expert", None),
            P(),
            P("expert", "dp", None, None),
            P("expert", "dp", None),
            P("expert", "dp"),
        ),
        out_specs=(
            P("expert", "dp"),
            P("expert", None),
            P("expert", "dp"),
            P("expert", "dp", None, None),
        ),
        check_vma=False,
    )
```

```python
import jax
import jax.numpy as jnp
from jax import lax
from jax.sharding import PartitionSpec as P

F32 = jnp.float32
BF16 = jnp.bfloat16


def shards(tokens, routes, gates, counts, w_gate_up, w_down, cotangent):
    experts = lax.axis_size("expert")
    rows, width = tokens.shape
    top = routes.shape[1]
    cap = min(rows, 2 * rows * top // experts)
    slots = experts * cap
    ff = w_down.shape[2]
    pair_weight = w_gate_up[0]
    down_weight = w_down[0]

    slot_id = jnp.arange(slots, dtype=jnp.int32)
    slot_expert = slot_id // cap
    slot_pos = slot_id % cap
    named = routes[:, :, None] == slot_expert[None, None, :]
    member = jnp.any(named, axis=1).astype(BF16)
    earlier = jnp.tril(jnp.ones((rows, rows), BF16), -1)
    before = jnp.dot(earlier, member, preferred_element_type=F32)
    place = jnp.where(before == slot_pos[None, :].astype(F32), member, jnp.zeros((), BF16))
    gate_of = jnp.sum(jnp.where(named, gates[:, :, None], 0.0), axis=1) * place.astype(F32)
    gate_slot = jnp.sum(gate_of, axis=0)

    both = jnp.concatenate([tokens, cotangent], axis=1)
    picked = lax.dot_general(place, both, (((0,), (0,)), ((), ())), preferred_element_type=F32)
    scale = jnp.where(jnp.arange(2 * width)[None, :] < width, 1.0, gate_slot[:, None])
    outgoing = (picked * scale).astype(BF16).reshape(experts, cap, 2 * width)
    arrived = lax.all_to_all(outgoing, "expert", split_axis=0, concat_axis=0, tiled=True)
    arrived = arrived.reshape(slots, 2 * width)
    rows_in = arrived[:, :width]
    grad_rows = arrived[:, width:]

    pair_part = lax.dot_general(
        rows_in, pair_weight, (((1,), (0,)), ((), ())), preferred_element_type=F32
    )
    hidden_grad_part = jnp.dot(grad_rows, down_weight, preferred_element_type=F32)
    part = jnp.concatenate([pair_part, hidden_grad_part[:, None, :]], axis=1)
    sums = lax.psum_scatter(part, "dp", scatter_dimension=0, tiled=True)
    gate_part, up_part, hidden_grad = sums[:, 0], sums[:, 1], sums[:, 2]
    sig_gate = jax.nn.sigmoid(gate_part)
    silu_gate = gate_part * sig_gate
    hidden_value = silu_gate * up_part
    slope_term = sig_gate * (1.0 + gate_part * (1.0 - sig_gate))
    gate_dot = jnp.sum(hidden_value * hidden_grad, axis=1)
    hidden = hidden_value.astype(BF16)
    gate_grad_part = (hidden_grad * up_part * slope_term).astype(BF16)
    up_grad_part = (hidden_grad * silu_gate).astype(BF16)
    later_weight, _ = lax.optimization_barrier((pair_weight, part))
    flat_weight = later_weight.reshape(width, 2 * ff)
    pair_full = lax.all_gather(
        jnp.concatenate([gate_grad_part, up_grad_part], axis=1), "dp", axis=0, tiled=True
    )

    ranks = lax.axis_size("dp")
    side = 4
    strided = [[q + side * i for i in range(ranks // side)] for q in range(side)]
    nearby = [[side * i + q for q in range(side)] for i in range(ranks // side)]
    dot_hi = gate_dot.astype(BF16)
    dot_lo = (gate_dot - dot_hi.astype(F32)).astype(BF16)
    lane = jnp.arange(128)[None, :]
    dots = jnp.where(
        lane == 0, dot_hi[:, None], jnp.where(lane == 1, dot_lo[:, None], jnp.zeros((), BF16))
    )
    payload = jnp.concatenate([hidden, dots], axis=1)
    columns = lax.all_gather(payload, "dp", axis=0, tiled=True, axis_index_groups=strided)
    cut = ff // 2

    def near(value):
        got = lax.all_gather(value, "dp", axis=0, tiled=False, axis_index_groups=nearby)
        got = got.reshape(side, ranks // side, slots // ranks, value.shape[1])
        return got.transpose(1, 0, 2, 3).reshape(slots, value.shape[1])

    low = near(columns[:, :cut])
    high = near(columns[:, cut:])
    hidden_full = jnp.concatenate([low, high[:, : ff - cut]], axis=1)
    expert_out = lax.dot_general(
        hidden_full, down_weight, (((1,), (1,)), ((), ())), preferred_element_type=F32
    ).astype(BF16)

    def send_back(value):
        sent = value.reshape(experts, cap, value.shape[1])
        came = lax.all_to_all(sent, "expert", split_axis=0, concat_axis=0, tiled=True)
        return came.reshape(slots, value.shape[1])

    first_back = send_back(jnp.concatenate([expert_out, high[:, ff - cut :]], axis=1))
    out_back = first_back[:, :width]
    dot_back = jnp.sum(first_back[:, width:].astype(F32), axis=1)
    at_slot = place.astype(F32) * dot_back[None, :]
    gate_grad = jnp.sum(jnp.where(named, at_slot[:, None, :], 0.0), axis=2) / gates

    row_grad = lax.dot_general(
        pair_full, flat_weight, (((1,), (1,)), ((), ())), preferred_element_type=F32
    ).astype(BF16)
    grad_back = send_back(row_grad)

    shares = counts.astype(F32) / jnp.sum(counts.astype(F32))
    slot_share = jnp.repeat(shares, cap)[:, None]
    weighted_pair = (slot_share * pair_full.astype(F32)).astype(BF16)
    weighted_hidden = (slot_share * hidden_full.astype(F32)).astype(BF16)
    gate_update = lax.dot_general(
        rows_in, weighted_pair[:, :ff], (((0,), (0,)), ((), ())), preferred_element_type=F32
    ).astype(BF16)
    up_update = lax.dot_general(
        rows_in, weighted_pair[:, ff:], (((0,), (0,)), ((), ())), preferred_element_type=F32
    ).astype(BF16)
    down_update = lax.dot_general(
        grad_rows, weighted_hidden, (((0,), (0,)), ((), ())), preferred_element_type=F32
    ).astype(BF16)
    weight_grads = jnp.stack([gate_update, up_update, down_update], axis=1)

    gate_hi = gate_of.astype(BF16)
    gate_lo = (gate_of - gate_hi.astype(F32)).astype(BF16)
    combine = jnp.concatenate([gate_hi, gate_lo], axis=0)
    mixed_parts = jnp.dot(combine, out_back, preferred_element_type=F32)
    mixed = (mixed_parts[:rows] + mixed_parts[rows:]).astype(BF16)
    token_grad = jnp.dot(place, grad_back, preferred_element_type=F32).astype(BF16)
    return (mixed, gate_grad, token_grad, weight_grads[None])


def solution(mesh):
    return jax.shard_map(
        shards,
        mesh=mesh,
        in_specs=(
            P("expert", "dp"),
            P("expert", None),
            P("expert", None),
            P(),
            P("expert", "dp", None, None),
            P("expert", "dp", None),
            P("expert", "dp"),
        ),
        out_specs=(
            P("expert", "dp"),
            P("expert", None),
            P("expert", "dp"),
            P("expert", "dp", None, None),
        ),
        check_vma=False,
    )
```

```python
import jax
import jax.numpy as jnp
from jax import lax
from jax.sharding import PartitionSpec as P

F32 = jnp.float32
BF16 = jnp.bfloat16


def shards(tokens, routes, gates, counts, w_gate_up, w_down, cotangent):
    experts = lax.axis_size("expert")
    rows, width = tokens.shape
    top = routes.shape[1]
    cap = min(rows, 2 * rows * top // experts)
    slots = experts * cap
    ff = w_down.shape[2]
    pair_weight = w_gate_up[0]
    down_weight = w_down[0]

    slot_id = jnp.arange(slots, dtype=jnp.int32)
    slot_expert = slot_id // cap
    slot_pos = slot_id % cap
    named = routes[:, :, None] == slot_expert[None, None, :]
    member = jnp.any(named, axis=1).astype(BF16)
    earlier = jnp.tril(jnp.ones((rows, rows), BF16), -1)
    before = jnp.dot(earlier, member, preferred_element_type=F32)
    place = jnp.where(before == slot_pos[None, :].astype(F32), member, jnp.zeros((), BF16))
    gate_of = jnp.sum(jnp.where(named, gates[:, :, None], 0.0), axis=1) * place.astype(F32)
    gate_slot = jnp.sum(gate_of, axis=0)

    both = jnp.concatenate([tokens, cotangent], axis=1)
    picked = lax.dot_general(place, both, (((0,), (0,)), ((), ())), preferred_element_type=F32)
    scale = jnp.where(jnp.arange(2 * width)[None, :] < width, 1.0, gate_slot[:, None])
    outgoing = (picked * scale).astype(BF16).reshape(experts, cap, 2 * width)
    arrived = lax.all_to_all(outgoing, "expert", split_axis=0, concat_axis=0, tiled=True)
    arrived = arrived.reshape(slots, 2 * width)
    rows_in = arrived[:, :width]
    grad_rows = arrived[:, width:]

    pair_part = lax.dot_general(
        rows_in, pair_weight, (((1,), (0,)), ((), ())), preferred_element_type=F32
    )
    hidden_grad_part = jnp.dot(grad_rows, down_weight, preferred_element_type=F32)
    part = jnp.concatenate([pair_part, hidden_grad_part[:, None, :]], axis=1)
    sums = lax.psum_scatter(part, "dp", scatter_dimension=0, tiled=True)
    later_weight, later_counts, _ = lax.optimization_barrier((pair_weight, counts, part))
    flat_weight = later_weight.reshape(width, 2 * ff)
    shares = later_counts.astype(F32) / jnp.sum(later_counts.astype(F32))
    slot_share = jnp.repeat(shares, cap)[:, None]
    sums, flat_weight, slot_share = lax.optimization_barrier((sums, flat_weight, slot_share))
    gate_part, up_part, hidden_grad = sums[:, 0], sums[:, 1], sums[:, 2]
    sig_gate = jax.nn.sigmoid(gate_part)
    silu_gate = gate_part * sig_gate
    hidden_value = silu_gate * up_part
    slope_term = sig_gate * (1.0 + gate_part * (1.0 - sig_gate))
    gate_dot = jnp.sum(hidden_value * hidden_grad, axis=1)
    hidden = hidden_value.astype(BF16)
    gate_grad_part = (hidden_grad * up_part * slope_term).astype(BF16)
    up_grad_part = (hidden_grad * silu_gate).astype(BF16)
    pair_full = lax.all_gather(
        jnp.concatenate([gate_grad_part, up_grad_part], axis=1), "dp", axis=0, tiled=True
    )

    ranks = lax.axis_size("dp")
    side = 4
    strided = [[q + side * i for i in range(ranks // side)] for q in range(side)]
    nearby = [[side * i + q for q in range(side)] for i in range(ranks // side)]
    dot_hi = gate_dot.astype(BF16)
    dot_lo = (gate_dot - dot_hi.astype(F32)).astype(BF16)
    lane = jnp.arange(128)[None, :]
    dots = jnp.where(
        lane == 0, dot_hi[:, None], jnp.where(lane == 1, dot_lo[:, None], jnp.zeros((), BF16))
    )
    payload = jnp.concatenate([hidden, dots], axis=1)
    columns = lax.all_gather(payload, "dp", axis=0, tiled=True, axis_index_groups=strided)
    cut = ff // 2

    def near(value):
        got = lax.all_gather(value, "dp", axis=0, tiled=False, axis_index_groups=nearby)
        got = got.reshape(side, ranks // side, slots // ranks, value.shape[1])
        return got.transpose(1, 0, 2, 3).reshape(slots, value.shape[1])

    low = near(columns[:, :cut])
    high = near(columns[:, cut:])
    hidden_full = jnp.concatenate([low, high[:, : ff - cut]], axis=1)
    expert_out = lax.dot_general(
        hidden_full, down_weight, (((1,), (1,)), ((), ())), preferred_element_type=F32
    ).astype(BF16)

    def send_back(value):
        sent = value.reshape(experts, cap, value.shape[1])
        came = lax.all_to_all(sent, "expert", split_axis=0, concat_axis=0, tiled=True)
        return came.reshape(slots, value.shape[1])

    first_back = send_back(jnp.concatenate([expert_out, high[:, ff - cut :]], axis=1))
    row_grad = lax.dot_general(
        pair_full, flat_weight, (((1,), (1,)), ((), ())), preferred_element_type=F32
    ).astype(BF16)
    grad_back = send_back(row_grad)
    first_back, pair_full, _ = lax.optimization_barrier((first_back, pair_full, row_grad))
    out_back = first_back[:, :width]
    dot_back = jnp.sum(first_back[:, width:].astype(F32), axis=1)
    at_slot = place.astype(F32) * dot_back[None, :]
    gate_grad = jnp.sum(jnp.where(named, at_slot[:, None, :], 0.0), axis=2) / gates

    weighted_pair = (slot_share * pair_full.astype(F32)).astype(BF16)
    weighted_hidden = (slot_share * hidden_full.astype(F32)).astype(BF16)
    gate_update = lax.dot_general(
        rows_in, weighted_pair[:, :ff], (((0,), (0,)), ((), ())), preferred_element_type=F32
    ).astype(BF16)
    up_update = lax.dot_general(
        rows_in, weighted_pair[:, ff:], (((0,), (0,)), ((), ())), preferred_element_type=F32
    ).astype(BF16)
    down_update = lax.dot_general(
        grad_rows, weighted_hidden, (((0,), (0,)), ((), ())), preferred_element_type=F32
    ).astype(BF16)
    weight_grads = jnp.stack([gate_update, up_update, down_update], axis=1)

    gate_hi = gate_of.astype(BF16)
    gate_lo = (gate_of - gate_hi.astype(F32)).astype(BF16)
    combine = jnp.concatenate([gate_hi, gate_lo], axis=0)
    mixed_parts = jnp.dot(combine, out_back, preferred_element_type=F32)
    mixed = (mixed_parts[:rows] + mixed_parts[rows:]).astype(BF16)
    token_grad = jnp.dot(place, grad_back, preferred_element_type=F32).astype(BF16)
    return (mixed, gate_grad, token_grad, weight_grads[None])


def solution(mesh):
    return jax.shard_map(
        shards,
        mesh=mesh,
        in_specs=(
            P("expert", "dp"),
            P("expert", None),
            P("expert", None),
            P(),
            P("expert", "dp", None, None),
            P("expert", "dp", None),
            P("expert", "dp"),
        ),
        out_specs=(
            P("expert", "dp"),
            P("expert", None),
            P("expert", "dp"),
            P("expert", "dp", None, None),
        ),
        check_vma=False,
    )
```

```python
import jax
import jax.numpy as jnp
from jax import lax
from jax.sharding import PartitionSpec as P

F32 = jnp.float32
BF16 = jnp.bfloat16


def shards(tokens, routes, gates, counts, w_gate_up, w_down, cotangent):
    experts = lax.axis_size("expert")
    rows, width = tokens.shape
    top = routes.shape[1]
    cap = min(rows, 2 * rows * top // experts)
    slots = experts * cap
    ff = w_down.shape[2]
    pair_weight = w_gate_up[0]
    down_weight = w_down[0]

    slot_id = jnp.arange(slots, dtype=jnp.int32)
    slot_expert = slot_id // cap
    slot_pos = slot_id % cap
    named = routes[:, :, None] == slot_expert[None, None, :]
    member = jnp.any(named, axis=1).astype(BF16)
    earlier = jnp.tril(jnp.ones((rows, rows), BF16), -1)
    before = jnp.dot(earlier, member, preferred_element_type=F32)
    place = jnp.where(before == slot_pos[None, :].astype(F32), member, jnp.zeros((), BF16))
    gate_of = jnp.sum(jnp.where(named, gates[:, :, None], 0.0), axis=1) * place.astype(F32)
    gate_slot = jnp.sum(gate_of, axis=0)

    both = jnp.concatenate([tokens, cotangent], axis=1)
    picked = lax.dot_general(place, both, (((0,), (0,)), ((), ())), preferred_element_type=F32)
    scale = jnp.where(jnp.arange(2 * width)[None, :] < width, 1.0, gate_slot[:, None])
    outgoing = (picked * scale).astype(BF16).reshape(experts, cap, 2 * width)
    arrived = lax.all_to_all(outgoing, "expert", split_axis=0, concat_axis=0, tiled=True)
    arrived = arrived.reshape(slots, 2 * width)
    rows_in = arrived[:, :width]
    grad_rows = arrived[:, width:]

    pair_part = lax.dot_general(
        rows_in, pair_weight, (((1,), (0,)), ((), ())), preferred_element_type=F32
    )
    sums = lax.psum_scatter(pair_part, "dp", scatter_dimension=0, tiled=True)

    ranks = lax.axis_size("dp")
    side = 4
    far = ranks // side
    strided = [[q + side * i for i in range(far)] for q in range(side)]
    nearby = [[side * i + q for q in range(side)] for i in range(far)]

    hidden_grad_part = jnp.dot(grad_rows, down_weight, preferred_element_type=F32).astype(BF16)
    blocks = hidden_grad_part.reshape(far, side, slots // ranks, ff).transpose(1, 0, 2, 3)
    close = lax.all_to_all(
        blocks, "dp", split_axis=0, concat_axis=0, axis_index_groups=nearby, tiled=True
    )
    close = close.astype(F32)
    close = ((close[0] + close[1]) + (close[2] + close[3])).astype(BF16)
    wide = lax.all_to_all(
        close, "dp", split_axis=0, concat_axis=0, axis_index_groups=strided, tiled=True
    )
    hidden_grad = jnp.sum(wide.astype(F32), axis=0)

    later_weight, later_counts, _ = lax.optimization_barrier((pair_weight, counts, pair_part))
    flat_weight = later_weight.reshape(width, 2 * ff)
    shares = later_counts.astype(F32) / jnp.sum(later_counts.astype(F32))
    slot_share = jnp.repeat(shares, cap)[:, None]
    sums, flat_weight, slot_share, hidden_grad = lax.optimization_barrier(
        (sums, flat_weight, slot_share, hidden_grad)
    )
    gate_part, up_part = sums[:, 0], sums[:, 1]
    sig_gate = jax.nn.sigmoid(gate_part)
    silu_gate = gate_part * sig_gate
    hidden_value = silu_gate * up_part
    slope_term = sig_gate * (1.0 + gate_part * (1.0 - sig_gate))
    gate_dot = jnp.sum(hidden_value * hidden_grad, axis=1)
    hidden = hidden_value.astype(BF16)
    gate_grad_part = (hidden_grad * up_part * slope_term).astype(BF16)
    up_grad_part = (hidden_grad * silu_gate).astype(BF16)
    pair_full = lax.all_gather(
        jnp.concatenate([gate_grad_part, up_grad_part], axis=1), "dp", axis=0, tiled=True
    )

    dot_hi = gate_dot.astype(BF16)
    dot_lo = (gate_dot - dot_hi.astype(F32)).astype(BF16)
    lane = jnp.arange(128)[None, :]
    dots = jnp.where(
        lane == 0, dot_hi[:, None], jnp.where(lane == 1, dot_lo[:, None], jnp.zeros((), BF16))
    )
    payload = jnp.concatenate([hidden, dots], axis=1)
    columns = lax.all_gather(payload, "dp", axis=0, tiled=True, axis_index_groups=strided)
    cut = ff // 2

    def near(value):
        got = lax.all_gather(value, "dp", axis=0, tiled=False, axis_index_groups=nearby)
        got = got.reshape(side, far, slots // ranks, value.shape[1])
        return got.transpose(1, 0, 2, 3).reshape(slots, value.shape[1])

    low = near(columns[:, :cut])
    high = near(columns[:, cut:])
    hidden_full = jnp.concatenate([low, high[:, : ff - cut]], axis=1)
    expert_out = lax.dot_general(
        hidden_full, down_weight, (((1,), (1,)), ((), ())), preferred_element_type=F32
    ).astype(BF16)

    def send_back(value):
        sent = value.reshape(experts, cap, value.shape[1])
        came = lax.all_to_all(sent, "expert", split_axis=0, concat_axis=0, tiled=True)
        return came.reshape(slots, value.shape[1])

    first_back = send_back(jnp.concatenate([expert_out, high[:, ff - cut :]], axis=1))
    row_grad = lax.dot_general(
        pair_full, flat_weight, (((1,), (1,)), ((), ())), preferred_element_type=F32
    ).astype(BF16)
    grad_back = send_back(row_grad)
    first_back, _ = lax.optimization_barrier((first_back, row_grad))
    pair_full, _ = lax.optimization_barrier((pair_full, row_grad))
    out_back = first_back[:, :width]
    dot_back = jnp.sum(first_back[:, width:].astype(F32), axis=1)
    at_slot = place.astype(F32) * dot_back[None, :]
    gate_grad = jnp.sum(jnp.where(named, at_slot[:, None, :], 0.0), axis=2) / gates

    weighted_pair = (slot_share * pair_full.astype(F32)).astype(BF16)
    weighted_hidden = (slot_share * hidden_full.astype(F32)).astype(BF16)
    gate_update = lax.dot_general(
        rows_in, weighted_pair[:, :ff], (((0,), (0,)), ((), ())), preferred_element_type=F32
    ).astype(BF16)
    up_update = lax.dot_general(
        rows_in, weighted_pair[:, ff:], (((0,), (0,)), ((), ())), preferred_element_type=F32
    ).astype(BF16)
    down_update = lax.dot_general(
        grad_rows, weighted_hidden, (((0,), (0,)), ((), ())), preferred_element_type=F32
    ).astype(BF16)
    weight_grads = jnp.stack([gate_update, up_update, down_update], axis=1)

    gate_hi = gate_of.astype(BF16)
    gate_lo = (gate_of - gate_hi.astype(F32)).astype(BF16)
    combine = jnp.concatenate([gate_hi, gate_lo], axis=0)
    mixed_parts = jnp.dot(combine, out_back, preferred_element_type=F32)
    mixed = (mixed_parts[:rows] + mixed_parts[rows:]).astype(BF16)
    token_grad = jnp.dot(place, grad_back, preferred_element_type=F32).astype(BF16)
    return (mixed, gate_grad, token_grad, weight_grads[None])


def solution(mesh):
    return jax.shard_map(
        shards,
        mesh=mesh,
        in_specs=(
            P("expert", "dp"),
            P("expert", None),
            P("expert", None),
            P(),
            P("expert", "dp", None, None),
            P("expert", "dp", None),
            P("expert", "dp"),
        ),
        out_specs=(
            P("expert", "dp"),
            P("expert", None),
            P("expert", "dp"),
            P("expert", "dp", None, None),
        ),
        check_vma=False,
    )
```

```python
import jax
import jax.numpy as jnp
from jax import lax
from jax.sharding import PartitionSpec as P

F32 = jnp.float32
BF16 = jnp.bfloat16


def shards(tokens, routes, gates, counts, w_gate_up, w_down, cotangent):
    experts = lax.axis_size("expert")
    rows, width = tokens.shape
    top = routes.shape[1]
    cap = min(rows, 2 * rows * top // experts)
    slots = experts * cap
    ff = w_down.shape[2]
    pair_weight = w_gate_up[0]
    down_weight = w_down[0]

    routes_by = routes.T
    gates_by = gates.T
    slot_id = jnp.arange(slots, dtype=jnp.int32)[:, None]
    slot_expert = slot_id // cap
    slot_pos = (slot_id % cap).astype(F32)
    named = routes_by[:, None, :] == slot_expert[None]
    member = jnp.any(named, axis=0).astype(BF16)
    earlier = jnp.triu(jnp.ones((rows, rows), BF16), 1)
    before = jnp.dot(member, earlier, preferred_element_type=F32)
    place = jnp.where(before == slot_pos, member, jnp.zeros((), BF16))
    gate_of = jnp.sum(jnp.where(named, gates_by[:, None, :], 0.0), axis=0) * place.astype(F32)
    gate_slot = jnp.sum(gate_of, axis=1, keepdims=True)

    both = jnp.concatenate([tokens, cotangent], axis=1)
    picked = jnp.dot(place, both, preferred_element_type=F32)
    scale = jnp.where(jnp.arange(2 * width)[None, :] < width, 1.0, gate_slot)
    outgoing = (picked * scale).astype(BF16).reshape(experts, cap, 2 * width)
    arrived = lax.all_to_all(outgoing, "expert", split_axis=0, concat_axis=0, tiled=True)
    arrived = arrived.reshape(slots, 2 * width)
    rows_in = arrived[:, :width]
    grad_rows = arrived[:, width:]

    pair_part = lax.dot_general(
        rows_in, pair_weight, (((1,), (0,)), ((), ())), preferred_element_type=F32
    )
    hidden_grad_part = jnp.dot(grad_rows, down_weight, preferred_element_type=F32)
    part = jnp.concatenate([pair_part, hidden_grad_part[:, None, :]], axis=1)
    sums = lax.psum_scatter(part, "dp", scatter_dimension=0, tiled=True)
    later_weight, later_counts, _ = lax.optimization_barrier((pair_weight, counts, part))
    flat_weight = later_weight.reshape(width, 2 * ff).T
    shares = later_counts.astype(F32) / jnp.sum(later_counts.astype(F32))
    slot_share = jnp.repeat(shares, cap)[:, None]
    sums, flat_weight, slot_share = lax.optimization_barrier((sums, flat_weight, slot_share))
    gate_part, up_part, hidden_grad = sums[:, 0], sums[:, 1], sums[:, 2]
    sig_gate = jax.nn.sigmoid(gate_part)
    silu_gate = gate_part * sig_gate
    hidden_value = silu_gate * up_part
    slope_term = sig_gate * (1.0 + gate_part * (1.0 - sig_gate))
    gate_dot = jnp.sum(hidden_value * hidden_grad, axis=1)
    hidden = hidden_value.astype(BF16)
    gate_grad_part = (hidden_grad * up_part * slope_term).astype(BF16)
    up_grad_part = (hidden_grad * silu_gate).astype(BF16)
    pair_full = lax.all_gather(
        jnp.concatenate([gate_grad_part, up_grad_part], axis=1), "dp", axis=0, tiled=True
    )

    ranks = lax.axis_size("dp")
    side = 4
    strided = [[q + side * i for i in range(ranks // side)] for q in range(side)]
    nearby = [[side * i + q for q in range(side)] for i in range(ranks // side)]
    dot_hi = gate_dot.astype(BF16)
    dot_lo = (gate_dot - dot_hi.astype(F32)).astype(BF16)
    lane = jnp.arange(128)[None, :]
    dots = jnp.where(
        lane == 0, dot_hi[:, None], jnp.where(lane == 1, dot_lo[:, None], jnp.zeros((), BF16))
    )
    payload = jnp.concatenate([hidden, dots], axis=1)
    columns = lax.all_gather(payload, "dp", axis=0, tiled=True, axis_index_groups=strided)
    cut = ff // 2

    def near(value):
        got = lax.all_gather(value, "dp", axis=0, tiled=False, axis_index_groups=nearby)
        got = got.reshape(side, ranks // side, slots // ranks, value.shape[1])
        return got.transpose(1, 0, 2, 3).reshape(slots, value.shape[1])

    low = near(columns[:, :cut])
    high = near(columns[:, cut:])
    hidden_full = jnp.concatenate([low, high[:, : ff - cut]], axis=1)
    expert_out = lax.dot_general(
        hidden_full, down_weight, (((1,), (1,)), ((), ())), preferred_element_type=F32
    ).astype(BF16)

    def send_back(value):
        sent = value.reshape(experts, cap, value.shape[1])
        came = lax.all_to_all(sent, "expert", split_axis=0, concat_axis=0, tiled=True)
        return came.reshape(slots, value.shape[1])

    first_back = send_back(jnp.concatenate([expert_out, high[:, ff - cut :]], axis=1))
    row_grad = jnp.dot(pair_full, flat_weight, preferred_element_type=F32).astype(BF16)
    grad_back = send_back(row_grad)
    first_back, _ = lax.optimization_barrier((first_back, row_grad))
    pair_full, _ = lax.optimization_barrier((pair_full, row_grad))
    out_back = first_back[:, :width]
    dot_back = jnp.sum(first_back[:, width:].astype(F32), axis=1)
    at_slot = place.astype(F32) * dot_back[:, None]
    gate_grad = (jnp.sum(jnp.where(named, at_slot[None], 0.0), axis=1) / gates_by).T

    weighted_pair = (slot_share * pair_full.astype(F32)).astype(BF16)
    weighted_hidden = (slot_share * hidden_full.astype(F32)).astype(BF16)
    gate_update = lax.dot_general(
        rows_in, weighted_pair[:, :ff], (((0,), (0,)), ((), ())), preferred_element_type=F32
    ).astype(BF16)
    up_update = lax.dot_general(
        rows_in, weighted_pair[:, ff:], (((0,), (0,)), ((), ())), preferred_element_type=F32
    ).astype(BF16)
    down_update = lax.dot_general(
        grad_rows, weighted_hidden, (((0,), (0,)), ((), ())), preferred_element_type=F32
    ).astype(BF16)
    weight_grads = jnp.stack([gate_update, up_update, down_update], axis=1)

    gate_hi = gate_of.astype(BF16)
    gate_lo = (gate_of - gate_hi.astype(F32)).astype(BF16)
    combine = jnp.concatenate([gate_hi, gate_lo], axis=1)
    mixed_parts = lax.dot_general(
        combine, out_back, (((0,), (0,)), ((), ())), preferred_element_type=F32
    )
    mixed = (mixed_parts[:rows] + mixed_parts[rows:]).astype(BF16)
    token_grad = lax.dot_general(
        place, grad_back, (((0,), (0,)), ((), ())), preferred_element_type=F32
    ).astype(BF16)
    return (mixed, gate_grad, token_grad, weight_grads[None])


def solution(mesh):
    return jax.shard_map(
        shards,
        mesh=mesh,
        in_specs=(
            P("expert", "dp"),
            P("expert", None),
            P("expert", None),
            P(),
            P("expert", "dp", None, None),
            P("expert", "dp", None),
            P("expert", "dp"),
        ),
        out_specs=(
            P("expert", "dp"),
            P("expert", None),
            P("expert", "dp"),
            P("expert", "dp", None, None),
        ),
        check_vma=False,
    )
```

```python
import jax
import jax.numpy as jnp
from jax import lax
from jax.sharding import PartitionSpec as P

F32 = jnp.float32
BF16 = jnp.bfloat16


def shards(tokens, routes, gates, counts, w_gate_up, w_down, cotangent):
    experts = lax.axis_size("expert")
    rows, width = tokens.shape
    top = routes.shape[1]
    cap = min(rows, 2 * rows * top // experts)
    slots = experts * cap
    ff = w_down.shape[2]
    pair_weight = w_gate_up[0]
    down_weight = w_down[0]

    routes_by = routes.T
    gates_by = gates.T
    slot_id = jnp.arange(slots, dtype=jnp.int32)[:, None]
    slot_expert = slot_id // cap
    slot_pos = (slot_id % cap).astype(F32)
    named = routes_by[:, None, :] == slot_expert[None]
    member = jnp.any(named, axis=0).astype(BF16)
    earlier = jnp.triu(jnp.ones((rows, rows), BF16), 1)
    before = jnp.dot(member, earlier, preferred_element_type=F32)
    place = jnp.where(before == slot_pos, member, jnp.zeros((), BF16))
    gate_of = jnp.sum(jnp.where(named, gates_by[:, None, :], 0.0), axis=0) * place.astype(F32)
    gate_slot = jnp.sum(gate_of, axis=1, keepdims=True)

    both = jnp.concatenate([tokens, cotangent], axis=1)
    picked = jnp.dot(place, both, preferred_element_type=F32)
    scale = jnp.where(jnp.arange(2 * width)[None, :] < width, 1.0, gate_slot)
    outgoing = (picked * scale).astype(BF16).reshape(experts, cap, 2 * width)
    arrived = lax.all_to_all(outgoing, "expert", split_axis=0, concat_axis=0, tiled=True)
    arrived = arrived.reshape(slots, 2 * width)
    rows_in = arrived[:, :width]
    grad_rows = arrived[:, width:]

    pair_part = lax.dot_general(
        rows_in, pair_weight, (((1,), (0,)), ((), ())), preferred_element_type=F32
    )
    hidden_grad_part = jnp.dot(grad_rows, down_weight, preferred_element_type=F32)
    part = jnp.concatenate([pair_part, hidden_grad_part[:, None, :]], axis=1)
    sums = lax.psum_scatter(part, "dp", scatter_dimension=0, tiled=True)
    later_weight, later_counts, later_down, _ = lax.optimization_barrier(
        (pair_weight, counts, down_weight, part)
    )
    through = jnp.concatenate(
        [
            jnp.pad(later_down, ((0, 0), (0, 128))),
            jnp.pad(jnp.eye(128, dtype=BF16), ((0, 0), (ff, 0))),
        ],
        axis=0,
    )
    flat_weight = later_weight.reshape(width, 2 * ff).T
    shares = later_counts.astype(F32) / jnp.sum(later_counts.astype(F32))
    slot_share = jnp.repeat(shares, cap)[:, None]
    sums, flat_weight, slot_share, through = lax.optimization_barrier(
        (sums, flat_weight, slot_share, through)
    )
    gate_part, up_part, hidden_grad = sums[:, 0], sums[:, 1], sums[:, 2]
    sig_gate = jax.nn.sigmoid(gate_part)
    silu_gate = gate_part * sig_gate
    hidden_value = silu_gate * up_part
    slope_term = sig_gate * (1.0 + gate_part * (1.0 - sig_gate))
    gate_dot = jnp.sum(hidden_value * hidden_grad, axis=1)
    hidden = hidden_value.astype(BF16)
    gate_grad_part = (hidden_grad * up_part * slope_term).astype(BF16)
    up_grad_part = (hidden_grad * silu_gate).astype(BF16)
    pair_full = lax.all_gather(
        jnp.concatenate([gate_grad_part, up_grad_part], axis=1), "dp", axis=0, tiled=True
    )

    ranks = lax.axis_size("dp")
    side = 4
    strided = [[q + side * i for i in range(ranks // side)] for q in range(side)]
    nearby = [[side * i + q for q in range(side)] for i in range(ranks // side)]
    dot_hi = gate_dot.astype(BF16)
    dot_lo = (gate_dot - dot_hi.astype(F32)).astype(BF16)
    lane = jnp.arange(128)[None, :]
    dots = jnp.where(
        lane == 0, dot_hi[:, None], jnp.where(lane == 1, dot_lo[:, None], jnp.zeros((), BF16))
    )
    payload = jnp.concatenate([hidden, dots], axis=1)
    columns = lax.all_gather(payload, "dp", axis=0, tiled=True, axis_index_groups=strided)
    cut = ff // 2

    def near(value):
        got = lax.all_gather(value, "dp", axis=0, tiled=False, axis_index_groups=nearby)
        got = got.reshape(side, ranks // side, slots // ranks, value.shape[1])
        return got.transpose(1, 0, 2, 3).reshape(slots, value.shape[1])

    low = near(columns[:, :cut])
    high = near(columns[:, cut:])
    hidden_dots = jnp.concatenate([low, high], axis=1)
    hidden_full = hidden_dots[:, :ff]
    expert_out = lax.dot_general(
        hidden_dots, through, (((1,), (1,)), ((), ())), preferred_element_type=F32
    ).astype(BF16)

    def send_back(value):
        sent = value.reshape(experts, cap, value.shape[1])
        came = lax.all_to_all(sent, "expert", split_axis=0, concat_axis=0, tiled=True)
        return came.reshape(slots, value.shape[1])

    first_back = send_back(expert_out)
    row_grad = jnp.dot(pair_full, flat_weight, preferred_element_type=F32).astype(BF16)
    grad_back = send_back(row_grad)
    first_back, _ = lax.optimization_barrier((first_back, row_grad))
    pair_full, _ = lax.optimization_barrier((pair_full, row_grad))
    out_back = first_back[:, :width]
    dot_back = jnp.sum(first_back[:, width:].astype(F32), axis=1)
    at_slot = place.astype(F32) * dot_back[:, None]
    gate_grad = (jnp.sum(jnp.where(named, at_slot[None], 0.0), axis=1) / gates_by).T

    weighted_pair = (slot_share * pair_full.astype(F32)).astype(BF16)
    weighted_hidden = (slot_share * hidden_full.astype(F32)).astype(BF16)
    gate_update = lax.dot_general(
        rows_in, weighted_pair[:, :ff], (((0,), (0,)), ((), ())), preferred_element_type=F32
    ).astype(BF16)
    up_update = lax.dot_general(
        rows_in, weighted_pair[:, ff:], (((0,), (0,)), ((), ())), preferred_element_type=F32
    ).astype(BF16)
    down_update = lax.dot_general(
        grad_rows, weighted_hidden, (((0,), (0,)), ((), ())), preferred_element_type=F32
    ).astype(BF16)
    weight_grads = jnp.stack([gate_update, up_update, down_update], axis=1)

    gate_hi = gate_of.astype(BF16)
    gate_lo = (gate_of - gate_hi.astype(F32)).astype(BF16)
    combine = jnp.concatenate([gate_hi, gate_lo], axis=1)
    mixed_parts = lax.dot_general(
        combine, out_back, (((0,), (0,)), ((), ())), preferred_element_type=F32
    )
    mixed = (mixed_parts[:rows] + mixed_parts[rows:]).astype(BF16)
    token_grad = lax.dot_general(
        place, grad_back, (((0,), (0,)), ((), ())), preferred_element_type=F32
    ).astype(BF16)
    return (mixed, gate_grad, token_grad, weight_grads[None])


def solution(mesh):
    return jax.shard_map(
        shards,
        mesh=mesh,
        in_specs=(
            P("expert", "dp"),
            P("expert", None),
            P("expert", None),
            P(),
            P("expert", "dp", None, None),
            P("expert", "dp", None),
            P("expert", "dp"),
        ),
        out_specs=(
            P("expert", "dp"),
            P("expert", None),
            P("expert", "dp"),
            P("expert", "dp", None, None),
        ),
        check_vma=False,
    )
```
